256 devices in a mesh: row: 8 (over x, core), col: 32 (over z, y).
Axes of the slice: x: 4, y: 4, z: 8, core: 2. Of those that a mesh axis runs over, the one named last changes fastest.
Arguments:
- amplitudes: bfloat16 [6144, 73728], P(('row', 'col')), may hold values from -6 to 6
- integrals: bfloat16 [1152, 73728], P('col', 'row'), may hold values from -0.0234375 to 0.0234375
- block_sizes: int32 [8], replicated, may hold values from 57 to 96, as said below
- window_irreps: int32 [2], replicated, may hold values from 0 to 7
Outputs:
- ladder: float32 [6144, 1152], P(('row', 'col'))
The draws below stay inside these ranges and needn't reach their ends.
Inputs may be any that keep to these rules, and one draw needn't show every extreme that they name: `block_sizes`: each irrep block holds at least 57 orbitals, its first slots; at least one block is full.
All inputs are finite; a program needn't handle non-finite values.
Results may differ from the reference program's by a relative error of at most 0.0003.
Values may be sent and summed in bfloat16 or wider, within the bound.
A program may use at most 128 MiB of HBM per device.

```python
import jax
import jax.numpy as jnp
from jax import lax

NIRR = 8
NB = 96
NA = 12
PAIRS = 6144
CD = 73728
AB = 1152
N_ROW = 8
N_COL = 32


def draw_block_sizes(key, part):
    key_sizes = jax.random.fold_in(key, 11)
    key_full = jax.random.fold_in(key, 23)
    drawn_sizes = jax.random.randint(key_sizes, (NIRR,), NB * 3 // 5, NB + 1, dtype=jnp.int32)
    full_irrep = jax.random.randint(key_full, (), 0, NIRR, dtype=jnp.int32)
    return jnp.where(jnp.arange(NIRR, dtype=jnp.int32) == full_irrep, NB, drawn_sizes).astype(jnp.int32)


def level_of(rng, dims, pieces, low, largest):
    factor_of, own = 1.0, jax.random.fold_in(rng, 6)
    for axis_at, blocks in pieces:
        heights = jnp.exp(jax.random.uniform(jax.random.fold_in(own, axis_at), (blocks,), jnp.float32, low / len(pieces), largest / len(pieces)))
        factor_of = factor_of * jnp.repeat(heights, dims[axis_at] // blocks).reshape([-1 if axis == axis_at else 1 for axis in range(len(dims))])
    return factor_of


def scatter_about(rng, dims, scale, limit, cuts=(), kind=jnp.bfloat16):
    loudness = level_of(rng, dims, cuts, -0.22, 0.18) if cuts else 1.0
    values = jax.random.normal(rng, dims, jnp.float32) * scale * loudness
    return jnp.minimum(jnp.maximum(values, -limit), limit).astype(kind)


def setup_inputs(seed: int = 0) -> dict:
    streams_of = jax.random.split(jax.random.key(seed), 5)
    amplitudes = scatter_about(streams_of[0], (PAIRS, CD), 1.0, 6.0, ((0, 256),))
    integrals = scatter_about(streams_of[1], (AB, CD), CD ** -0.5, 0.0234375, ((0, 32), (1, 8)))
    block_sizes = draw_block_sizes(jax.random.fold_in(streams_of[4], 71), 0)
    window_irreps = jax.random.randint(streams_of[3], (2,), 0, NIRR).astype(jnp.int32)
    return {"amplitudes": amplitudes, "integrals": integrals, "block_sizes": block_sizes, "window_irreps": window_irreps}


def size_lookup(block_sizes, irrep_ids):
    options = jnp.arange(NIRR, dtype=jnp.int32)
    return jnp.sum(jnp.where(irrep_ids[:, None] == options[None, :], block_sizes[None, :], 0), axis=1).astype(jnp.int32)


def live_columns(block_sizes, pair_irrep):
    pair_index = jnp.arange(NIRR * NB * NB, dtype=jnp.int32)
    irrep_c = pair_index // (NB * NB)
    slot_c = (pair_index // NB) % NB
    slot_d = pair_index % NB
    irrep_d = jnp.bitwise_xor(irrep_c, pair_irrep)
    return (slot_c < size_lookup(block_sizes, irrep_c)) & (slot_d < size_lookup(block_sizes, irrep_d))


def reference(amplitudes, integrals, block_sizes, window_irreps):
    live_mask = live_columns(block_sizes, window_irreps[0]).astype(jnp.bfloat16)
    panel = integrals * live_mask[None, :]
    pair_blocks = amplitudes.reshape(N_ROW * N_COL // 8, PAIRS * 8 // (N_ROW * N_COL), NIRR * NB * NB)

    def one_block(pair_block):
        return lax.dot_general(pair_block, panel, (((1,), (1,)), ((), ())), preferred_element_type=jnp.float32)

    raw = lax.map(one_block, pair_blocks).reshape(PAIRS, NA * NB)
    size_b = block_sizes[window_irreps[1]]
    slot_mask = (jnp.arange(NA * NB, dtype=jnp.int32) % NB) < size_b
    return jnp.where(slot_mask[None, :], raw, jnp.float32(0.0))
```

```python
import functools

import jax
import jax.numpy as jnp
from jax import lax
from jax.experimental import pallas as pl
from jax.experimental.pallas import tpu as pltpu
from jax.sharding import PartitionSpec as P

NIRR = 8
NB = 96
MESH = pl.DeviceIdType.MESH
LANES = 128
QUAD = 4 * NB
NQ = 24
WT = 5
KT = 18
UNROLL = 6
SPARE = 24
PEERS = [(1, 0), (0, 1), (3, 0), (0, 3), (2, 0), (0, 2), (1, 1), (3, 3), (1, 3), (3, 1),
         (2, 1), (1, 2), (2, 3), (3, 2), (2, 2)]


def selection(size):
    i = lax.broadcasted_iota(jnp.int32, (QUAD, QUAD), 0)
    k = (i >= NB).astype(jnp.int32) + (i >= 2 * NB).astype(jnp.int32) + (i >= 3 * NB).astype(jnp.int32)
    d = i - NB * k
    target = jnp.where(d < size, k * size + d, -1)
    j = lax.broadcasted_iota(jnp.int32, (QUAD, QUAD), 1)
    return jnp.where(j == target, 1.0, 0.0).astype(jnp.bfloat16)


def moved(first, second, following, lane, shift, rest):
    run = pltpu.roll(jnp.where(lane >= shift, first, second), (LANES - shift) & 127, 1)
    return jnp.where(lane < rest, run, pltpu.roll(following, rest & 127, 1))


def tile_at(t):
    return pl.ds(pl.multiple_of(t * LANES, LANES), LANES)


def pack_kernel(sizes, window, a_hbm, b_hbm, a_out, b_out, place, width,
                a_v, b_v, y_a, x_b, y_b, a_pack, b_pack, s_load, s_store):
    row, col = lax.axis_index("row"), lax.axis_index("col")
    core, chip = row % 2, (row // 2) * 4 + col % 4
    load_b = pltpu.make_async_copy(b_hbm, b_v, s_load.at[8])
    load_b.start()
    loads = []
    for h in range(NIRR):
        part = pl.ds(h * NB * NB, NB * NB)
        loads.append(pltpu.make_async_copy(a_hbm.at[:, part], a_v.at[:, part], s_load.at[h]))
        loads[-1].start()
    g = window[0]

    def irrep(h):
        size = sizes[h ^ g]
        live = sizes[h] * size
        return size, live, (live + LANES - 1) // LANES

    base, total = [], [0, 0]
    for h in range(NIRR):
        base.append(total[h % 2])
        total[h % 2] = total[h % 2] + irrep(h)[2]
    width[0] = jnp.maximum(total[0] + 15, total[1] + 15) // 16
    mine = 0
    for h in range(NIRR):
        mine = jnp.where(row == h, base[h], mine)
    ends = jnp.where(core == 0, total[0], total[1])

    @pl.loop(0, KT)
    def _(i):
        n = 16 * i + chip
        which, start = jnp.int32(0), jnp.int32(0)
        for k in range(1, 4):
            first = jnp.where(core == 0, base[2 * k], base[2 * k + 1])
            which = jnp.where(n >= first, k, which)
            start = jnp.where(n >= first, first, start)
        place[0, i] = which
        place[1, i] = jnp.minimum((n - start) // 16, WT - 1)
        place[2, i] = (n < ends).astype(jnp.int32)

    def step(quad, offset, quad_width):
        offset = offset + LANES
        over = offset >= quad_width
        return jnp.where(over, quad + 1, quad), jnp.where(over, offset - quad_width, offset)

    load_b.wait()
    for q in range(NQ):
        x_b[q, 0:36, :] = b_v[:, q * QUAD:(q + 1) * QUAD].astype(jnp.float32)
    size, live, _ = irrep(row)
    y_b[3 * NQ] = jnp.zeros((40, LANES), jnp.float32)
    packed_b = jnp.dot(
        x_b[...].reshape(NQ * 40, QUAD).astype(jnp.bfloat16), selection(size),
        preferred_element_type=jnp.float32)
    for q in range(NQ):
        for t in range(3):
            y_b[3 * q + t] = packed_b[40 * q:40 * q + 40, t * LANES:(t + 1) * LANES]
    lane_b = lax.broadcasted_iota(jnp.int32, (40, LANES), 1)

    @pl.loop(0, 16 * WT // 8, init_carry=(jnp.int32(0), jnp.int32(0)))
    def _(group, carry):
        quad, offset = carry
        for u in range(8):
            m = 8 * group + u
            t = jnp.minimum(3 * quad + offset // LANES, 3 * NQ - 1)
            after = jnp.minimum(3 * quad + 3, 3 * NQ)
            v = moved(y_b[t], y_b[t + 1], y_b[after], lane_b, offset % LANES, 4 * size - offset)
            b_pack[(mine + m) % 16, m // 16] = jnp.where(lane_b < live - m * LANES, v, 0.0).astype(jnp.bfloat16)
            quad, offset = step(quad, offset, 4 * size)
        return quad, offset

    stores = [pltpu.make_async_copy(b_pack, b_out, s_store.at[2])]
    stores[0].start()

    for t in range(SPARE):
        y_a[NIRR * NQ * 3 + t] = jnp.zeros((24, LANES), jnp.float32)
    for h in range(NIRR):
        loads[h].wait()

    @pl.loop(0, NIRR)
    def _(h):
        wide = [a_v[:, pl.ds(pl.multiple_of(h * NB * NB + q * QUAD, LANES), QUAD)].astype(jnp.float32)
                for q in range(NQ)]
        packed = jnp.dot(jnp.concatenate(wide, axis=0).astype(jnp.bfloat16), selection(irrep(h)[0]),
                         preferred_element_type=jnp.float32)
        for q in range(NQ):
            for t in range(3):
                y_a[(h * NQ + q) * 3 + t] = packed[24 * q:24 * q + 24, t * LANES:(t + 1) * LANES]

    lane_a = lax.broadcasted_iota(jnp.int32, (24, LANES), 1)
    for half in range(2):
        @pl.loop(0, 4, init_carry=jnp.int32(0))
        def _(k, first):
            h = 2 * k + half
            size, _, count = irrep(h)

            @pl.loop(0, (count + UNROLL - 1) // UNROLL, init_carry=(h * NQ, jnp.int32(0)))
            def _(group, carry):
                quad, offset = carry
                for u in range(UNROLL):
                    n = first + UNROLL * group + u
                    t = 3 * quad + offset // LANES
                    v = moved(y_a[t], y_a[t + 1], y_a[3 * quad + 3], lane_a, offset % LANES, 4 * size - offset)
                    a_pack[half, n % 16, :, tile_at(n // 16)] = v.astype(jnp.bfloat16)
                    quad, offset = step(quad, offset, 4 * size)
                return quad, offset

            return first + count

        @pl.loop(total[half], 16 * KT)
        def _(n):
            a_pack[half, n % 16, :, tile_at(n // 16)] = jnp.zeros((24, LANES), jnp.bfloat16)

        stores.append(pltpu.make_async_copy(a_pack.at[half, :, :, 0:KT * LANES], a_out.at[half], s_store.at[half]))
        stores[-1].start()
    for c in stores:
        c.wait()


def pack_call(sizes, window, amplitudes, integrals):
    bf, f32 = jnp.bfloat16, jnp.float32
    smem = pl.BlockSpec(memory_space=pltpu.SMEM)
    hbm = pl.BlockSpec(memory_space=pl.ANY)
    return pl.pallas_call(
        pack_kernel,
        out_shape=(jax.ShapeDtypeStruct((2, 16, 24, KT * LANES), bf), jax.ShapeDtypeStruct((16, WT, 40, LANES), bf),
                   jax.ShapeDtypeStruct((3, KT), jnp.int32), jax.ShapeDtypeStruct((1,), jnp.int32)),
        in_specs=[smem, smem, hbm, hbm],
        out_specs=(hbm, hbm, smem, smem),
        scratch_shapes=[
            pltpu.VMEM((24, NIRR * NB * NB), bf),
            pltpu.VMEM((36, NB * NB), bf),
            pltpu.VMEM((NIRR * NQ * 3 + SPARE, 24, LANES), f32),
            pltpu.VMEM((NQ, 40, QUAD), f32),
            pltpu.VMEM((NQ * 3 + 1, 40, LANES), f32),
            pltpu.VMEM((2, 16, 24, (KT + 1) * LANES), bf),
            pltpu.VMEM((16, WT, 40, LANES), bf),
            pltpu.SemaphoreType.DMA((9,)), pltpu.SemaphoreType.DMA((3,)),
        ],
        compiler_params=pltpu.CompilerParams(vmem_limit_bytes=60 * 2**20),
    )(sizes, window, amplitudes, integrals)


def kernel(kt, place, window, sizes, a_hbm, b_hbm, o_ref,
           b_recv, dense, a_recv, a_mat, b_main, b_rest, c_part, c_in1, c_sum, c_in2, c_out,
           s_own, s_bs, s_br, s_as, s_ar, s_zs, s_zr, s_rs, s_rr, s_ks, s_kr, s_c1s, s_c1r, s_c2s, s_c2r):
    row, col = lax.axis_index("row"), lax.axis_index("col")
    x, core = row // 2, row % 2
    z, y = col // 4, col % 4
    chip = x * 4 + y

    def plane(dx, dy):
        px, py = (x + dx) % 4, (y + dy) % 4
        return (px * 2 + core, z * 4 + py), px * 4 + py

    up = (row, ((z + 1) % 8) * 4 + y)
    down = (row, ((z + 7) % 8) * 4 + y)
    sibling = (x * 2 + 1 - core, col)

    used = pl.ds(0, kt * LANES)
    own = [pltpu.make_async_copy(b_hbm.at[chip], b_recv.at[chip], s_own.at[0])]
    for half in range(2):
        own.append(pltpu.make_async_copy(a_hbm.at[half, chip, :, used], a_recv.at[half, chip], s_own.at[1 + half]))
    for c in own:
        c.start()

    barrier = pltpu.get_barrier_semaphore()
    for who in [plane(*p)[0] for p in PEERS] + [up, down, sibling]:
        pl.semaphore_signal(barrier, 1, device_id=who, device_id_type=MESH)
    pl.semaphore_wait(barrier, len(PEERS) + 3)

    def remote(src, dst, send, recv, who):
        return pltpu.make_async_remote_copy(src, dst, send, recv, device_id=who, device_id_type=MESH)

    b_copies, a_copies = [], [[], []]
    for i, (dx, dy) in enumerate(PEERS):
        who, target = plane(dx, dy)
        b_copies.append(remote(b_hbm.at[target], b_recv.at[chip], s_bs.at[i], s_br.at[i], who))
        b_copies[-1].start()
    for half in range(2):
        for i, (dx, dy) in enumerate(PEERS):
            who, target = plane(dx, dy)
            a_copies[half].append(remote(a_hbm.at[half, target, :, used], a_recv.at[half, chip],
                                         s_as.at[half, i], s_ar.at[half, i], who))
            a_copies[half][-1].start()
    for c in own:
        c.wait()

    for c in b_copies:
        c.wait()

    @pl.loop(0, kt)
    def _(i):
        px, k, valid = place[0, i], place[1, i], place[2, i]
        for py in range(4):
            v = b_recv[px * 4 + py, k].astype(jnp.float32)
            dense[36 * py:36 * py + 36, :] = jnp.where(valid > 0, v, 0.0)[0:36, :]
        d = dense[...].astype(jnp.bfloat16)
        b_main[0, core, :, tile_at(i)] = d[0:128]
        b_rest[core, pl.ds(pl.multiple_of(16 * z, 16), 16), tile_at(i)] = d[128:144]

    def main_copies(step):
        rows_up = pl.ds(0, 128) if step < 3 else pl.ds(0, 64)
        rows_down = pl.ds(0, 128) if step < 3 else pl.ds(64, 64)
        a, b = (8 - step) % 8, (7 - step) % 8
        return (remote(b_main.at[a, core, rows_up], b_main.at[b, core, rows_up],
                       s_zs.at[0, step], s_zr.at[0, step], up),
                remote(b_main.at[step, core, rows_down], b_main.at[step + 1, core, rows_down],
                       s_zs.at[1, step], s_zr.at[1, step], down))

    def rest_copies(step):
        at_up = pl.ds(pl.multiple_of(16 * ((z + 8 - step) % 8), 16), 16)
        at_down = pl.ds(pl.multiple_of(16 * ((z + step) % 8), 16), 16)
        out = [remote(b_rest.at[core, at_up], b_rest.at[core, at_up], s_rs.at[0, step], s_rr.at[0, step], up)]
        if step < 3:
            out.append(remote(b_rest.at[core, at_down], b_rest.at[core, at_down],
                              s_rs.at[1, step], s_rr.at[1, step], down))
        return out

    def share(r):
        return remote(b_main.at[r, core], b_main.at[r, core], s_ks.at[r], s_kr.at[r], sibling)

    def start(copies):
        for c in copies:
            c.start()
        return copies

    def got(copies):
        for c in copies:
            c.wait_recv()

    main, rest, shared = [], [], {}
    rest.append(start(rest_copies(0)))
    main.append(start(main_copies(0)))
    shared[0] = share(0)
    shared[0].start()

    def next_rest(step):
        got(rest[step - 1])
        rest.append(start(rest_copies(step)))

    def next_main(step):
        got(main[step - 1])
        main.append(start(main_copies(step)))
        for r in (step, 8 - step):
            shared[r] = share(r)
            shared[r].start()

    def repack(half):
        got(a_copies[half])

        @pl.loop(0, 8)
        def _(s):
            v = a_recv[half, pl.ds(2 * s, 2)].astype(jnp.float32)
            a_mat[half, pl.ds(pl.multiple_of(48 * s, 48), 48), :] = v.reshape(48, kt * LANES).astype(jnp.bfloat16)

    next_rest(1)
    next_rest(2)
    next_rest(3)
    next_main(1)
    repack(0)
    next_main(2)
    next_main(3)
    repack(1)
    got(rest[3])
    share_rest = remote(b_rest.at[core], b_rest.at[core], s_ks.at[8], s_kr.at[8], sibling)
    share_rest.start()

    def product(r):
        total = None
        for half in range(2):
            right = b_main[r, half] if r < 8 else b_rest[half]
            v = lax.dot_general(a_mat[half], right, (((1,), (1,)), ((), ())), preferred_element_type=jnp.float32)
            total = v if total is None else total + v
        c_part[r] = total.reshape(4, 4, 24, LANES)

    first, second = {}, {}

    def line(r, k, phase):
        along_x = (r % 2 == 0) == (phase == 1)
        return plane(k, 0)[0] if along_x else plane(0, k)[0]

    def send_first(r):
        first[r] = []
        for k in (1, 3, 2):
            if r % 2 == 0:
                src = c_part.at[r, (x + k) % 4]
            else:
                src = c_part.at[r, :, (y + k) % 4]
            first[r].append(remote(src, c_in1.at[r, k - 1], s_c1s.at[r, k - 1], s_c1r.at[r, k - 1], line(r, k, 1)))
        start(first[r])

    def send_second(r):
        got(first[r])
        own = c_part[r, x] if r % 2 == 0 else c_part[r, :, y]
        c_sum[r] = own + c_in1[r, 0] + c_in1[r, 1] + c_in1[r, 2]
        second[r] = []
        for k in (1, 3, 2):
            src = c_sum.at[r, (y + k) % 4] if r % 2 == 0 else c_sum.at[r, (x + k) % 4]
            second[r].append(remote(src, c_in2.at[r, k - 1], s_c2s.at[r, k - 1], s_c2r.at[r, k - 1], line(r, k, 2)))
        start(second[r])

    def finish(r):
        got(second[r])
        own = c_sum[r, y] if r % 2 == 0 else c_sum[r, x]
        at = (z + r) % 8 if r < 8 else 8
        c_out[at] = own + c_in2[r, 0] + c_in2[r, 1] + c_in2[r, 2]

    def tile(r):
        if r < 8:
            shared[r].wait_recv()
        else:
            share_rest.wait_recv()
        product(r)
        send_first(r)

    for r in (0, 1, 7, 2, 6):
        tile(r)
    tile(8)
    for r in (3, 5):
        tile(r)
    for r in (0, 1, 7, 2, 6, 8):
        send_second(r)
    got(main[3])
    shared[4] = share(4)
    shared[4].start()
    tile(4)
    for r in (3, 5):
        send_second(r)
    for r in (0, 1, 7, 2, 6, 8):
        finish(r)
    send_second(4)
    for r in (3, 5, 4):
        finish(r)
    size_b = jnp.int32(0)
    for h in range(NIRR):
        size_b = jnp.where(window[1] == h, sizes[h], size_b)
    for t in range(8):
        o_ref[:, 144 * t:144 * t + 128] = c_out[t]
        o_ref[:, 144 * t + 128:144 * t + 144] = c_out[8, :, 16 * t:16 * t + 16]
    slot = lax.broadcasted_iota(jnp.int32, (24, 8 * 144), 1)
    o_ref[...] = jnp.where(slot % NB < size_b, o_ref[...], 0.0)
    for group in rest + main + a_copies + list(first.values()) + list(second.values()):
        for c in group:
            c.wait_send()
    for c in list(shared.values()) + [share_rest]:
        c.wait_send()


def ladder_call(kt, collective_id, place, window, sizes, a_packed, b_packed):
    kh = kt * LANES
    bf, f32 = jnp.bfloat16, jnp.float32
    dma = pltpu.SemaphoreType.DMA
    smem = pl.BlockSpec(memory_space=pltpu.SMEM)
    hbm = pl.BlockSpec(memory_space=pl.ANY)
    return pl.pallas_call(
        functools.partial(kernel, kt),
        out_shape=jax.ShapeDtypeStruct((24, 8 * 144), f32),
        in_specs=[smem] * 3 + [hbm] * 2,
        out_specs=pl.BlockSpec(memory_space=pltpu.VMEM),
        scratch_shapes=[
            pltpu.VMEM((16, WT, 40, LANES), bf),
            pltpu.VMEM((144, LANES), f32),
            pltpu.VMEM((2, 16, 24, kh), bf),
            pltpu.VMEM((2, 384, kh), bf),
            pltpu.VMEM((8, 2, 128, kh), bf),
            pltpu.VMEM((2, 128, kh), bf),
            pltpu.VMEM((9, 4, 4, 24, LANES), f32),
            pltpu.VMEM((9, 3, 4, 24, LANES), f32),
            pltpu.VMEM((9, 4, 24, LANES), f32),
            pltpu.VMEM((9, 3, 24, LANES), f32),
            pltpu.VMEM((9, 24, LANES), f32),
            dma((3,)), dma((15,)), dma((15,)), dma((2, 15)), dma((2, 15)),
            dma((2, 4)), dma((2, 4)), dma((2, 4)), dma((2, 4)), dma((9,)), dma((9,)),
            dma((9, 3)), dma((9, 3)), dma((9, 3)), dma((9, 3)),
        ],
        compiler_params=pltpu.CompilerParams(
            collective_id=collective_id, has_side_effects=True, vmem_limit_bytes=60 * 2**20),
    )(place, window, sizes, a_packed, b_packed)


def shards(amplitudes, integrals, block_sizes, window_irreps):
    a_packed, b_packed, place, width = pack_call(block_sizes, window_irreps, amplitudes, integrals)
    return ladder_call(KT, 0, place, window_irreps, block_sizes, a_packed, b_packed)


def solution(mesh):
    placed = (P(("row", "col"), None), P("col", "row"), P(), P())
    return jax.shard_map(
        shards, mesh=mesh, in_specs=placed, out_specs=P(("row", "col"), None), check_vma=False
    )
```

```python
import functools

import jax
import jax.numpy as jnp
from jax import lax
from jax.experimental import pallas as pl
from jax.experimental.pallas import tpu as pltpu
from jax.sharding import PartitionSpec as P

NIRR = 8
NB = 96
MESH = pl.DeviceIdType.MESH
LANES = 128
QUAD = 4 * NB
NQ = 24
WT = 5
KT = 18
EARLY = 2
FIELDS = 5
WIDTHS = (12, 13, 15, 18)

def selection(size):
    i = lax.broadcasted_iota(jnp.int32, (QUAD, QUAD), 0)
    k = (i >= NB).astype(jnp.int32) + (i >= 2 * NB).astype(jnp.int32) + (i >= 3 * NB).astype(jnp.int32)
    d = i - NB * k
    target = jnp.where(d < size, k * size + d, -1)
    j = lax.broadcasted_iota(jnp.int32, (QUAD, QUAD), 1)
    return jnp.where(j == target, 1.0, 0.0).astype(jnp.bfloat16)


def moved(first, second, following, lane, shift, rest):
    run = pltpu.roll(jnp.where(lane >= shift, first, second), (LANES - shift) & 127, 1)
    return jnp.where(lane < rest, run, pltpu.roll(following, rest & 127, 1))


def tile_at(t):
    return pl.ds(pl.multiple_of(t * LANES, LANES), LANES)


def deal_kernel(sizes, window, b_hbm, b_out, table, width, b_v, x_b, y_b, b_pack, s_load):
    row = lax.axis_index("row")
    load_b = pltpu.make_async_copy(b_hbm, b_v, s_load)
    load_b.start()
    g = window[0]
    size = [sizes[h ^ g] for h in range(NIRR)]
    live = [sizes[h] * size[h] for h in range(NIRR)]
    tiles = [(live[h] + LANES - 1) // LANES for h in range(NIRR)]
    full = [jnp.maximum(tiles[h] // 16, EARLY) for h in range(NIRR)]
    left = [jnp.maximum(tiles[h] - 16 * full[h], 0) for h in range(NIRR)]
    start = [None] * NIRR
    all_full, all_left = [0, 0], [0, 0]
    for h in range(NIRR):
        start[h] = all_left[h % 2]
        all_full[h % 2] = all_full[h % 2] + full[h]
        all_left[h % 2] = all_left[h % 2] + left[h]
    slots = [all_full[p] + (all_left[p] + 15) // 16 for p in range(2)]
    width[0] = jnp.maximum(slots[0], slots[1])

    line = lax.broadcasted_iota(jnp.int32, (8, LANES), 0)
    lane = lax.broadcasted_iota(jnp.int32, (8, LANES), 1)
    fields = [jnp.zeros((8, LANES), jnp.int32)] * FIELDS
    for half in range(2):
        entry = (line - 3 * half) * LANES + lane
        slot, chip = entry >> 4, entry & 15
        which, k = slot & 3, slot >> 2
        m = 16 * k + chip
        good = slot < all_full[half]
        at = jnp.int32(4 * EARLY)
        for later in range(EARLY, WT):
            for i in range(4):
                has = full[2 * i + half] > later
                hit = (slot == jnp.where(has, at, -1))
                which, k, m = jnp.where(hit, i, which), jnp.where(hit, later, k), jnp.where(hit, 16 * later + chip, m)
                at = at + has.astype(jnp.int32)
        order = 16 * (slot - all_full[half]) + chip
        order = jnp.where(slot >= all_full[half], order, -1)
        for i in range(4):
            h = 2 * i + half
            hit = (order >= start[h]) & (order < start[h] + left[h])
            which, k = jnp.where(hit, i, which), jnp.where(hit, full[h], k)
            m = jnp.where(hit, 16 * full[h] + order - start[h], m)
        good = good | ((order >= 0) & (order < all_left[half]))
        which, k, m = jnp.where(good, which, 0), jnp.where(good, k, 0), jnp.where(good, m, 0)
        wide = 4 * size[half]
        for i in range(1, 4):
            wide = jnp.where(which == i, 4 * size[2 * i + half], jnp.broadcast_to(wide, (8, LANES)))
        position = m * LANES
        quad = ((position.astype(jnp.float32) + 0.5) / wide.astype(jnp.float32)).astype(jnp.int32)
        offset = position - quad * wide
        quad = quad + (2 * which + half) * NQ
        values = [3 * quad + (offset >> 7), 3 * quad + 3, offset & 127, wide - offset,
                  which * 8 + k + jnp.where(good, 64, 0)]
        here = (line >= 3 * half) & (line < 3 * half + 3)
        fields = [jnp.where(here, v, f) for v, f in zip(values, fields)]
    for i in range(FIELDS):
        table[8 * i:8 * i + 8, :] = fields[i]

    def mine(values):
        out = values[0]
        for h in range(1, NIRR):
            out = jnp.where(row == h, values[h], out)
        return out

    my_size, my_live, my_full, my_start = mine(size), mine(live), mine(full), mine(start)
    load_b.wait()
    for q in range(NQ):
        x_b[q, 0:36, :] = b_v[:, q * QUAD:(q + 1) * QUAD].astype(jnp.float32)
    y_b[3 * NQ] = jnp.zeros((40, LANES), jnp.float32)
    packed_b = jnp.dot(
        x_b[...].reshape(NQ * 40, QUAD).astype(jnp.bfloat16), selection(my_size),
        preferred_element_type=jnp.float32)
    for q in range(NQ):
        for t in range(3):
            y_b[3 * q + t] = packed_b[40 * q:40 * q + 40, t * LANES:(t + 1) * LANES]
    lane_b = lax.broadcasted_iota(jnp.int32, (40, LANES), 1)

    @pl.loop(0, 16 * WT // 8, init_carry=(jnp.int32(0), jnp.int32(0)))
    def _(group, carry):
        quad, offset = carry
        for u in range(8):
            m = 8 * group + u
            t = jnp.minimum(3 * quad + offset // LANES, 3 * NQ - 1)
            after = jnp.minimum(3 * quad + 3, 3 * NQ)
            v = moved(y_b[t], y_b[t + 1], y_b[after], lane_b, offset % LANES, 4 * my_size - offset)
            chip = (m + jnp.where(m >= 16 * my_full, my_start, 0)) % 16
            b_pack[chip, m // 16] = jnp.where(lane_b < my_live - m * LANES, v, 0.0).astype(jnp.bfloat16)
            offset = offset + LANES
            over = offset >= 4 * my_size
            quad, offset = jnp.where(over, quad + 1, quad), jnp.where(over, offset - 4 * my_size, offset)
        return quad, offset

    store = pltpu.make_async_copy(b_pack, b_out, s_load)
    store.start()
    store.wait()


def deal_call(sizes, window, integrals):
    bf, f32 = jnp.bfloat16, jnp.float32
    smem = pl.BlockSpec(memory_space=pltpu.SMEM)
    hbm = pl.BlockSpec(memory_space=pl.ANY)
    return pl.pallas_call(
        deal_kernel,
        out_shape=(jax.ShapeDtypeStruct((16, WT, 40, LANES), bf),
                   jax.ShapeDtypeStruct((8 * FIELDS, LANES), jnp.int32), jax.ShapeDtypeStruct((1,), jnp.int32)),
        in_specs=[smem, smem, hbm],
        out_specs=(hbm, pl.BlockSpec(memory_space=pltpu.VMEM), smem),
        scratch_shapes=[
            pltpu.VMEM((36, NB * NB), bf),
            pltpu.VMEM((NQ, 40, QUAD), f32),
            pltpu.VMEM((NQ * 3 + 1, 40, LANES), f32),
            pltpu.VMEM((16, WT, 40, LANES), bf),
            pltpu.SemaphoreType.DMA,
        ],
        compiler_params=pltpu.CompilerParams(vmem_limit_bytes=60 * 2**20),
    )(sizes, window, integrals)


def kernel(kt, table, window, sizes, a_hbm, b_hbm, o_ref,
           a_v, y_a, chosen, a_send, b_first, b_second, dense, a_recv, a_mat, b_main, c_part, c_in1, c_sum, c_in2, c_out,
           s_load, s_bs, s_br, s_as, s_ar, s_zs, s_zr, s_rs, s_rr, s_ks, s_kr, s_c1s, s_c1r, s_c2s, s_c2r):
    row, col = lax.axis_index("row"), lax.axis_index("col")
    x, core = row // 2, row % 2
    z, y = col // 4, col % 4
    chip = x * 4 + y

    def plane(i):
        step = (7 * i) % 16
        px, py = (x + step // 4) % 4, (y + step) % 4
        return (px * 2 + core, z * 4 + py), px * 4 + py

    up = (row, ((z + 1) % 8) * 4 + y)
    down = (row, ((z + 7) % 8) * 4 + y)
    sibling = (x * 2 + 1 - core, col)

    tiles_of = (pl.ds(0, EARLY), pl.ds(EARLY, WT - EARLY))
    b_recv = (b_first, b_second)
    own_b = [pltpu.make_async_copy(b_hbm.at[chip, tiles_of[i]], b_recv[i].at[chip], s_load.at[8 + i]) for i in range(2)]
    for c in own_b:
        c.start()

    def load(h):
        part = pl.ds(pl.multiple_of(h * NB * NB, LANES), NB * NB)
        return pltpu.make_async_copy(a_hbm.at[:, part], a_v.at[:, part], s_load.at[h])

    @pl.loop(0, NIRR)
    def _(h):
        load(h).start()

    barrier = pltpu.get_barrier_semaphore()

    @pl.loop(1, 16)
    def _(i):
        pl.semaphore_signal(barrier, 1, device_id=plane(i)[0], device_id_type=MESH)

    for who in (up, down, sibling):
        pl.semaphore_signal(barrier, 1, device_id=who, device_id_type=MESH)
    pl.semaphore_wait(barrier, 18)

    def remote(src, dst, send, recv, who):
        return pltpu.make_async_remote_copy(src, dst, send, recv, device_id=who, device_id_type=MESH)

    def start(copies):
        for c in copies:
            c.start()
        return copies

    def got(copies):
        for c in copies:
            c.wait_recv()

    def b_copy(chunk, i):
        who, target = plane(i)
        return remote(b_hbm.at[target, tiles_of[chunk]], b_recv[chunk].at[chip], s_bs.at[chunk, i], s_br.at[chunk, i], who)

    for chunk in range(2):
        pl.loop(1, 16)(lambda i: b_copy(chunk, i).start())

    y_a[3 * NIRR * NQ] = jnp.zeros((24, LANES), jnp.float32)

    @pl.loop(0, NIRR)
    def _(h):
        load(h).wait()
        chosen[...] = selection(sizes[h ^ window[0]])

        @pl.loop(0, 3)
        def _(part):
            first = h * NQ + 8 * part
            wide = [a_v[:, pl.ds(pl.multiple_of((first + q) * QUAD, LANES), QUAD)].astype(jnp.float32)
                    for q in range(8)]
            packed = jnp.dot(jnp.concatenate(wide, axis=0).astype(jnp.bfloat16), chosen[...],
                             preferred_element_type=jnp.float32)
            for q in range(8):
                for t in range(3):
                    y_a[(first + q) * 3 + t] = packed[24 * q:24 * q + 24, t * LANES:(t + 1) * LANES]

    lane_a = lax.broadcasted_iota(jnp.int32, (24, LANES), 1)

    def pack_a(half, i, target):
        def one(k):
            line, lane = 3 * half + k // 8, (k % 8) * 16 + target
            t, after, shift, rest = (table[8 * f + line, lane] for f in range(4))
            v = moved(y_a[t], y_a[t + 1], y_a[after], lane_a, shift, rest)
            a_send[half, i, :, tile_at(k)] = v.astype(jnp.bfloat16)

        pl.loop(0, kt, unroll=kt // 2 if kt % 2 == 0 else kt // 3 if kt % 3 == 0 else kt)(one)

    def a_copy(half, i):
        who, target = plane(i)
        return remote(a_send.at[half, i], a_recv.at[half, chip], s_as.at[half, i], s_ar.at[half, i], who)

    def own_a(half):
        return pltpu.make_async_copy(a_send.at[half, 0], a_recv.at[half, chip], s_as.at[half, 0])

    def send_a(half):
        @pl.loop(1, 16)
        def _(i):
            pack_a(half, i, plane(i)[1])
            a_copy(half, i).start()

        pack_a(half, 0, chip)
        own_a(half).start()

    def lay_out(i, piece):
        for py in range(4):
            dense[36 * py:36 * py + 36, :] = piece(py)[0:36, :]
        d = dense[...].astype(jnp.bfloat16)
        b_main[0, core, :, tile_at(i)] = d[0:128]
        b_main[8, core, pl.ds(pl.multiple_of(16 * z, 16), 16), tile_at(i)] = d[128:144]

    def lay_out_first():
        own_b[0].wait()
        pl.loop(1, 16)(lambda i: b_copy(0, i).wait_recv())

        @pl.loop(0, 4 * EARLY)
        def _(i):
            lay_out(i, lambda py: b_first[(i % 4) * 4 + py, i // 4].astype(jnp.float32))

    def lay_out_second():
        own_b[1].wait()
        pl.loop(1, 16)(lambda i: b_copy(1, i).wait_recv())

        @pl.loop(4 * EARLY, kt)
        def _(i):
            code = table[32 + 3 * core + i // 8, (i % 8) * 16 + chip]
            px, k = (code >> 3) & 3, jnp.maximum((code & 7) - EARLY, 0)
            lay_out(i, lambda py: jnp.where(code >= 64, b_second[px * 4 + py, k].astype(jnp.float32), 0.0))

    early = 4 * EARLY
    chunks = (pl.ds(0, early * LANES), pl.ds(early * LANES, (kt - early) * LANES))

    def main_copies(step, chunk):
        rows_up = pl.ds(0, 128) if step < 3 else pl.ds(0, 64)
        rows_down = pl.ds(0, 128) if step < 3 else pl.ds(64, 64)
        a, b = (8 - step) % 8, (7 - step) % 8
        at = chunks[chunk]
        return (remote(b_main.at[a, core, rows_up, at], b_main.at[b, core, rows_up, at],
                       s_zs.at[0, step, chunk], s_zr.at[0, step, chunk], up),
                remote(b_main.at[step, core, rows_down, at], b_main.at[step + 1, core, rows_down, at],
                       s_zs.at[1, step, chunk], s_zr.at[1, step, chunk], down))

    def rest_copies(step):
        at_up = pl.ds(pl.multiple_of(16 * ((z + 8 - step) % 8), 16), 16)
        at_down = pl.ds(pl.multiple_of(16 * ((z + step) % 8), 16), 16)
        out = [remote(b_main.at[8, core, at_up], b_main.at[8, core, at_up], s_rs.at[0, step], s_rr.at[0, step], up)]
        if step < 3:
            out.append(remote(b_main.at[8, core, at_down], b_main.at[8, core, at_down],
                              s_rs.at[1, step], s_rr.at[1, step], down))
        return out

    main, rest = {}, []

    def share(r, chunk):
        at = chunks[chunk]
        return remote(b_main.at[r, core, :, at], b_main.at[r, core, :, at], s_ks.at[r, chunk], s_kr.at[r, chunk], sibling)

    def next_rest(step):
        if step:
            got(rest[step - 1])
        rest.append(start(rest_copies(step)))

    def next_main(step, chunk):
        if step:
            got(main[step - 1, chunk])
        main[step, chunk] = start(main_copies(step, chunk))
        for r in sorted({step, (8 - step) % 8}):
            share(r, chunk).start()

    def repack(half):
        own_a(half).wait()
        pl.loop(1, 16)(lambda i: a_copy(half, i).wait_recv())

        @pl.loop(0, 8)
        def _(s):
            v = a_recv[half, pl.ds(2 * s, 2)].astype(jnp.float32)
            a_mat[half, pl.ds(pl.multiple_of(48 * s, 48), 48), :] = v.reshape(48, kt * LANES).astype(jnp.bfloat16)

    def tile_of(u):
        by_distance = ((u + 1) // 2 * (2 * (u % 2) - 1) + 8) % 8
        return (1 - u // 7) * by_distance + u // 7 * 8 - u // 8 * 4

    def product(r):
        for chunk in range(2):
            share(r, chunk).wait_recv()
        total = None
        for half in range(2):
            v = lax.dot_general(a_mat[half], b_main[r, half], (((1,), (1,)), ((), ())),
                                preferred_element_type=jnp.float32)
            total = v if total is None else total + v
        total = total.reshape(4, 4, 24, LANES)
        odd = r % 2
        for i in range(4):
            for j in range(4):
                c_part[r, i + odd * (j - i), j + odd * (i - j)] = total[i, j]

    def line_peer(r, k, odd):
        return (((x + k * (1 - odd)) % 4) * 2 + core, z * 4 + (y + k * odd) % 4)

    def first_copies(r):
        odd = r % 2
        mine = x + odd * (y - x)
        return [remote(c_part.at[r, (mine + k) % 4], c_in1.at[r, k - 1], s_c1s.at[r, k - 1], s_c1r.at[r, k - 1],
                       line_peer(r, k, odd)) for k in (1, 3, 2)]

    def second_copies(r):
        odd = r % 2
        mine = y + odd * (x - y)
        return [remote(c_sum.at[r, (mine + k) % 4], c_in2.at[r, k - 1], s_c2s.at[r, k - 1], s_c2r.at[r, k - 1],
                       line_peer(r, k, 1 - odd)) for k in (1, 3, 2)]

    def send_second(r):
        got(first_copies(r))
        c_sum[r] = c_part[r, x + r % 2 * (y - x)] + c_in1[r, 0] + c_in1[r, 1] + c_in1[r, 2]
        start(second_copies(r))

    def finish(r):
        got(second_copies(r))
        total = c_sum[r, y + r % 2 * (x - y)] + c_in2[r, 0] + c_in2[r, 1] + c_in2[r, 2]
        c_out[r // 8 * 8 + (1 - r // 8) * ((z + r) % 8)] = total

    send_a(0)
    lay_out_first()
    next_main(0, 0)
    send_a(1)
    lay_out_second()
    next_main(0, 1)
    next_rest(0)
    next_main(1, 0)
    next_rest(1)
    next_main(1, 1)
    next_rest(2)
    next_main(2, 0)
    next_rest(3)
    next_main(2, 1)
    repack(0)
    next_main(3, 0)
    got(rest[3])
    for chunk in range(2):
        share(8, chunk).start()
    next_main(3, 1)
    repack(1)

    @pl.loop(0, 13)
    def _(u):
        @pl.when(u == 8)
        def _():
            for chunk in range(2):
                got(main[3, chunk])
                share(4, chunk).start()

        @pl.when(u < 9)
        def _():
            r = tile_of(u)
            product(r)
            start(first_copies(r))

        @pl.when((u >= 2) & (u < 11))
        def _():
            send_second(tile_of(u - 2))

        @pl.when(u >= 4)
        def _():
            finish(tile_of(u - 4))

    size_b = jnp.int32(0)
    for h in range(NIRR):
        size_b = jnp.where(window[1] == h, sizes[h], size_b)
    for t in range(8):
        o_ref[:, 144 * t:144 * t + 128] = c_out[t]
        o_ref[:, 144 * t + 128:144 * t + 144] = c_out[8, :, 16 * t:16 * t + 16]
    slot = lax.broadcasted_iota(jnp.int32, (24, 8 * 144), 1)
    o_ref[...] = jnp.where(slot % NB < size_b, o_ref[...], 0.0)

    @pl.loop(1, 16)
    def _(i):
        for half in range(2):
            a_copy(half, i).wait_send()
            b_copy(half, i).wait_send()

    @pl.loop(0, 9)
    def _(r):
        for c in first_copies(r) + second_copies(r) + [share(r, 0), share(r, 1)]:
            c.wait_send()

    for copies in rest + list(main.values()):
        for c in copies:
            c.wait_send()


def ladder_call(kt, collective_id, table, window, sizes, amplitudes, b_packed):
    kh = kt * LANES
    bf, f32 = jnp.bfloat16, jnp.float32
    dma = pltpu.SemaphoreType.DMA
    smem = pl.BlockSpec(memory_space=pltpu.SMEM)
    hbm = pl.BlockSpec(memory_space=pl.ANY)
    return pl.pallas_call(
        functools.partial(kernel, kt),
        out_shape=jax.ShapeDtypeStruct((24, 8 * 144), f32),
        in_specs=[smem] * 3 + [hbm] * 2,
        out_specs=pl.BlockSpec(memory_space=pltpu.VMEM),
        scratch_shapes=[
            pltpu.VMEM((24, NIRR * NB * NB), bf),
            pltpu.VMEM((NIRR * NQ * 3 + 1, 24, LANES), f32),
            pltpu.VMEM((QUAD, QUAD), bf),
            pltpu.VMEM((2, 16, 24, kh), bf),
            pltpu.VMEM((16, EARLY, 40, LANES), bf),
            pltpu.VMEM((16, WT - EARLY, 40, LANES), bf),
            pltpu.VMEM((144, LANES), f32),
            pltpu.VMEM((2, 16, 24, kh), bf),
            pltpu.VMEM((2, 384, kh), bf),
            pltpu.VMEM((9, 2, 128, kh), bf),
            pltpu.VMEM((9, 4, 4, 24, LANES), f32),
            pltpu.VMEM((9, 3, 4, 24, LANES), f32),
            pltpu.VMEM((9, 4, 24, LANES), f32),
            pltpu.VMEM((9, 3, 24, LANES), f32),
            pltpu.VMEM((9, 24, LANES), f32),
            dma((10,)), dma((2, 16)), dma((2, 16)), dma((2, 16)), dma((2, 16)),
            dma((2, 4, 2)), dma((2, 4, 2)), dma((2, 4)), dma((2, 4)), dma((9, 2)), dma((9, 2)),
            dma((9, 3)), dma((9, 3)), dma((9, 3)), dma((9, 3)),
        ],
        compiler_params=pltpu.CompilerParams(
            collective_id=collective_id, has_side_effects=True, vmem_limit_bytes=60 * 2**20),
    )(table, window, sizes, amplitudes, b_packed)


def shards(amplitudes, integrals, block_sizes, window_irreps):
    b_packed, table, width = deal_call(block_sizes, window_irreps, integrals)
    which = sum((width[0] > w).astype(jnp.int32) for w in WIDTHS[:-1])
    calls = [functools.partial(ladder_call, w, i) for i, w in enumerate(WIDTHS)]
    return lax.switch(which, calls, table, window_irreps, block_sizes, amplitudes, b_packed)


def solution(mesh):
    placed = (P(("row", "col"), None), P("col", "row"), P(), P())
    return jax.shard_map(
        shards, mesh=mesh, in_specs=placed, out_specs=P(("row", "col"), None), check_vma=False
    )
```

```python
import functools

import jax
import jax.numpy as jnp
from jax import lax
from jax.experimental import pallas as pl
from jax.experimental.pallas import tpu as pltpu
from jax.sharding import PartitionSpec as P

NIRR = 8
NB = 96
MESH = pl.DeviceIdType.MESH
LANES = 128
QUAD = 4 * NB
NQ = 24
WT = 5
KT = 18
EARLY = 2
FIELDS = 5
WIDTHS = (12, 13, 15, 18)

def selection(size):
    i = lax.broadcasted_iota(jnp.int32, (QUAD, QUAD), 0)
    k = (i >= NB).astype(jnp.int32) + (i >= 2 * NB).astype(jnp.int32) + (i >= 3 * NB).astype(jnp.int32)
    d = i - NB * k
    target = jnp.where(d < size, k * size + d, -1)
    j = lax.broadcasted_iota(jnp.int32, (QUAD, QUAD), 1)
    return jnp.where(j == target, 1.0, 0.0).astype(jnp.bfloat16)


def moved(first, second, following, lane, shift, rest):
    run = pltpu.roll(jnp.where(lane >= shift, first, second), (LANES - shift) & 127, 1)
    return jnp.where(lane < rest, run, pltpu.roll(following, rest & 127, 1))


def tile_at(t):
    return pl.ds(pl.multiple_of(t * LANES, LANES), LANES)


def deal_kernel(sizes, window, b_hbm, b_out, table, width, b_v, x_b, y_b, b_pack, s_load):
    row = lax.axis_index("row")
    load_b = pltpu.make_async_copy(b_hbm, b_v, s_load)
    load_b.start()
    g = window[0]
    size = [sizes[h ^ g] for h in range(NIRR)]
    live = [sizes[h] * size[h] for h in range(NIRR)]
    tiles = [(live[h] + LANES - 1) // LANES for h in range(NIRR)]
    full = [jnp.maximum(tiles[h] // 16, EARLY) for h in range(NIRR)]
    left = [jnp.maximum(tiles[h] - 16 * full[h], 0) for h in range(NIRR)]
    start = [None] * NIRR
    all_full, all_left = [0, 0], [0, 0]
    for h in range(NIRR):
        start[h] = all_left[h % 2]
        all_full[h % 2] = all_full[h % 2] + full[h]
        all_left[h % 2] = all_left[h % 2] + left[h]
    slots = [all_full[p] + (all_left[p] + 15) // 16 for p in range(2)]
    width[0] = jnp.maximum(slots[0], slots[1])

    line = lax.broadcasted_iota(jnp.int32, (8, LANES), 0)
    lane = lax.broadcasted_iota(jnp.int32, (8, LANES), 1)
    fields = [jnp.zeros((8, LANES), jnp.int32)] * FIELDS
    for half in range(2):
        entry = (line - 3 * half) * LANES + lane
        slot, chip = entry >> 4, entry & 15
        which, k = slot & 3, slot >> 2
        m = 16 * k + chip
        good = slot < all_full[half]
        at = jnp.int32(4 * EARLY)
        for later in range(EARLY, WT):
            for i in range(4):
                has = full[2 * i + half] > later
                hit = (slot == jnp.where(has, at, -1))
                which, k, m = jnp.where(hit, i, which), jnp.where(hit, later, k), jnp.where(hit, 16 * later + chip, m)
                at = at + has.astype(jnp.int32)
        order = 16 * (slot - all_full[half]) + chip
        order = jnp.where(slot >= all_full[half], order, -1)
        for i in range(4):
            h = 2 * i + half
            hit = (order >= start[h]) & (order < start[h] + left[h])
            which, k = jnp.where(hit, i, which), jnp.where(hit, full[h], k)
            m = jnp.where(hit, 16 * full[h] + order - start[h], m)
        good = good | ((order >= 0) & (order < all_left[half]))
        which, k, m = jnp.where(good, which, 0), jnp.where(good, k, 0), jnp.where(good, m, 0)
        wide = 4 * size[half]
        for i in range(1, 4):
            wide = jnp.where(which == i, 4 * size[2 * i + half], jnp.broadcast_to(wide, (8, LANES)))
        position = m * LANES
        quad = ((position.astype(jnp.float32) + 0.5) / wide.astype(jnp.float32)).astype(jnp.int32)
        offset = position - quad * wide
        quad = quad + (which + 4 * half) * NQ
        values = [3 * quad + (offset >> 7), 3 * quad + 3, offset & 127, wide - offset,
                  which * 8 + k + jnp.where(good, 64, 0)]
        here = (line >= 3 * half) & (line < 3 * half + 3)
        fields = [jnp.where(here, v, f) for v, f in zip(values, fields)]
    for i in range(FIELDS):
        table[8 * i:8 * i + 8, :] = fields[i]

    def mine(values):
        out = values[0]
        for h in range(1, NIRR):
            out = jnp.where(row == h, values[h], out)
        return out

    my_size, my_live, my_full, my_start = mine(size), mine(live), mine(full), mine(start)
    load_b.wait()
    for q in range(NQ):
        x_b[q, 0:36, :] = b_v[:, q * QUAD:(q + 1) * QUAD].astype(jnp.float32)
    y_b[3 * NQ] = jnp.zeros((40, LANES), jnp.float32)
    packed_b = jnp.dot(
        x_b[...].reshape(NQ * 40, QUAD).astype(jnp.bfloat16), selection(my_size),
        preferred_element_type=jnp.float32)
    for q in range(NQ):
        for t in range(3):
            y_b[3 * q + t] = packed_b[40 * q:40 * q + 40, t * LANES:(t + 1) * LANES]
    lane_b = lax.broadcasted_iota(jnp.int32, (40, LANES), 1)

    @pl.loop(0, 16 * WT // 8, init_carry=(jnp.int32(0), jnp.int32(0)))
    def _(group, carry):
        quad, offset = carry
        for u in range(8):
            m = 8 * group + u
            t = jnp.minimum(3 * quad + offset // LANES, 3 * NQ - 1)
            after = jnp.minimum(3 * quad + 3, 3 * NQ)
            v = moved(y_b[t], y_b[t + 1], y_b[after], lane_b, offset % LANES, 4 * my_size - offset)
            chip = (m + jnp.where(m >= 16 * my_full, my_start, 0)) % 16
            b_pack[chip, m // 16] = jnp.where(lane_b < my_live - m * LANES, v, 0.0).astype(jnp.bfloat16)
            offset = offset + LANES
            over = offset >= 4 * my_size
            quad, offset = jnp.where(over, quad + 1, quad), jnp.where(over, offset - 4 * my_size, offset)
        return quad, offset

    store = pltpu.make_async_copy(b_pack, b_out, s_load)
    store.start()
    store.wait()


def deal_call(sizes, window, integrals):
    bf, f32 = jnp.bfloat16, jnp.float32
    smem = pl.BlockSpec(memory_space=pltpu.SMEM)
    hbm = pl.BlockSpec(memory_space=pl.ANY)
    return pl.pallas_call(
        deal_kernel,
        out_shape=(jax.ShapeDtypeStruct((16, WT, 40, LANES), bf),
                   jax.ShapeDtypeStruct((8 * FIELDS, LANES), jnp.int32), jax.ShapeDtypeStruct((1,), jnp.int32)),
        in_specs=[smem, smem, hbm],
        out_specs=(hbm, pl.BlockSpec(memory_space=pltpu.VMEM), smem),
        scratch_shapes=[
            pltpu.VMEM((36, NB * NB), bf),
            pltpu.VMEM((NQ, 40, QUAD), f32),
            pltpu.VMEM((NQ * 3 + 1, 40, LANES), f32),
            pltpu.VMEM((16, WT, 40, LANES), bf),
            pltpu.SemaphoreType.DMA,
        ],
        compiler_params=pltpu.CompilerParams(vmem_limit_bytes=60 * 2**20),
    )(sizes, window, integrals)


def kernel(kt, table, window, sizes, a_hbm, b_hbm, o_ref,
           a_v, y_a, chosen, a_send, b_first, b_second, dense, a_recv, a_mat, b_main, c_part, c_in1, c_sum, c_in2, c_out,
           s_load, s_bs, s_br, s_as, s_ar, s_zs, s_zr, s_rs, s_rr, s_ks, s_kr, s_c1s, s_c1r, s_c2s, s_c2r):
    row, col = lax.axis_index("row"), lax.axis_index("col")
    x, core = row // 2, row % 2
    z, y = col // 4, col % 4
    chip = x * 4 + y

    def plane(i):
        step = (7 * i) % 16
        px, py = (x + step // 4) % 4, (y + step) % 4
        return (px * 2 + core, z * 4 + py), px * 4 + py

    up = (row, ((z + 1) % 8) * 4 + y)
    down = (row, ((z + 7) % 8) * 4 + y)
    sibling = (x * 2 + 1 - core, col)

    tiles_of = (pl.ds(0, EARLY), pl.ds(EARLY, WT - EARLY))
    b_recv = (b_first, b_second)
    own_b = [pltpu.make_async_copy(b_hbm.at[chip, tiles_of[i]], b_recv[i].at[chip], s_load.at[8 + i]) for i in range(2)]
    for c in own_b:
        c.start()

    def load(h):
        part = pl.ds(pl.multiple_of(h * NB * NB, LANES), NB * NB)
        return pltpu.make_async_copy(a_hbm.at[:, part], a_v.at[:, part], s_load.at[h])

    @pl.loop(0, NIRR)
    def _(i):
        load(2 * (i % 4) + i // 4).start()

    barrier = pltpu.get_barrier_semaphore()

    @pl.loop(1, 16)
    def _(i):
        pl.semaphore_signal(barrier, 1, device_id=plane(i)[0], device_id_type=MESH)

    for who in (up, down, sibling):
        pl.semaphore_signal(barrier, 1, device_id=who, device_id_type=MESH)
    pl.semaphore_wait(barrier, 18)

    def remote(src, dst, send, recv, who):
        return pltpu.make_async_remote_copy(src, dst, send, recv, device_id=who, device_id_type=MESH)

    def start(copies):
        for c in copies:
            c.start()
        return copies

    def got(copies):
        for c in copies:
            c.wait_recv()

    def b_copy(chunk, i):
        who, target = plane(i)
        return remote(b_hbm.at[target, tiles_of[chunk]], b_recv[chunk].at[chip], s_bs.at[chunk, i], s_br.at[chunk, i], who)

    for chunk in range(2):
        pl.loop(1, 16)(lambda i: b_copy(chunk, i).start())

    for half in range(2):
        y_a[12 * NQ * (half + 1)] = jnp.zeros((24, LANES), jnp.float32)

    def pack_quads(half):
        @pl.loop(0, 4)
        def _(i):
            h = 2 * i + half
            load(h).wait()
            chosen[...] = selection(sizes[h ^ window[0]])

            @pl.loop(0, 3)
            def _(part):
                first = h * NQ + 8 * part
                to = (4 * half + i) * NQ + 8 * part
                wide = [a_v[:, pl.ds(pl.multiple_of((first + q) * QUAD, LANES), QUAD)].astype(jnp.float32)
                        for q in range(8)]
                packed = jnp.dot(jnp.concatenate(wide, axis=0).astype(jnp.bfloat16), chosen[...],
                                 preferred_element_type=jnp.float32)
                for q in range(8):
                    for t in range(3):
                        y_a[(to + q) * 3 + t] = packed[24 * q:24 * q + 24, t * LANES:(t + 1) * LANES]

    lane_a = lax.broadcasted_iota(jnp.int32, (24, LANES), 1)

    def pack_a(half, i, target):
        def one(k):
            line, lane = 3 * half + k // 8, (k % 8) * 16 + target
            t, after, shift, rest = (table[8 * f + line, lane] for f in range(4))
            v = moved(y_a[t], y_a[t + 1], y_a[after], lane_a, shift, rest)
            a_send[half, i, :, tile_at(k)] = v.astype(jnp.bfloat16)

        pl.loop(0, kt, unroll=kt // 2 if kt % 2 == 0 else kt // 3 if kt % 3 == 0 else kt)(one)

    def a_copy(half, i):
        who, target = plane(i)
        return remote(a_send.at[half, i], a_recv.at[half, chip], s_as.at[half, i], s_ar.at[half, i], who)

    def own_a(half):
        return pltpu.make_async_copy(a_send.at[half, 0], a_recv.at[half, chip], s_as.at[half, 0])

    def send_a(half):
        @pl.loop(1, 16)
        def _(i):
            pack_a(half, i, plane(i)[1])
            a_copy(half, i).start()

        pack_a(half, 0, chip)
        own_a(half).start()

    def lay_out(i, piece):
        for py in range(4):
            dense[36 * py:36 * py + 36, :] = piece(py)[0:36, :]
        d = dense[...].astype(jnp.bfloat16)
        b_main[0, core, :, tile_at(i)] = d[0:128]
        b_main[8, core, pl.ds(pl.multiple_of(16 * z, 16), 16), tile_at(i)] = d[128:144]

    def lay_out_first():
        own_b[0].wait()
        pl.loop(1, 16)(lambda i: b_copy(0, i).wait_recv())

        @pl.loop(0, 4 * EARLY)
        def _(i):
            lay_out(i, lambda py: b_first[(i % 4) * 4 + py, i // 4].astype(jnp.float32))

    def lay_out_second():
        own_b[1].wait()
        pl.loop(1, 16)(lambda i: b_copy(1, i).wait_recv())

        @pl.loop(4 * EARLY, kt)
        def _(i):
            code = table[32 + 3 * core + i // 8, (i % 8) * 16 + chip]
            px, k = (code >> 3) & 3, jnp.maximum((code & 7) - EARLY, 0)
            lay_out(i, lambda py: jnp.where(code >= 64, b_second[px * 4 + py, k].astype(jnp.float32), 0.0))

    early = 4 * EARLY
    chunks = (pl.ds(0, early * LANES), pl.ds(early * LANES, (kt - early) * LANES))

    def main_copies(step, chunk):
        rows_up = pl.ds(0, 128) if step < 3 else pl.ds(0, 64)
        rows_down = pl.ds(0, 128) if step < 3 else pl.ds(64, 64)
        a, b = (8 - step) % 8, (7 - step) % 8
        at = chunks[chunk]
        return (remote(b_main.at[a, core, rows_up, at], b_main.at[b, core, rows_up, at],
                       s_zs.at[0, step, chunk], s_zr.at[0, step, chunk], up),
                remote(b_main.at[step, core, rows_down, at], b_main.at[step + 1, core, rows_down, at],
                       s_zs.at[1, step, chunk], s_zr.at[1, step, chunk], down))

    def rest_copies(step):
        at_up = pl.ds(pl.multiple_of(16 * ((z + 8 - step) % 8), 16), 16)
        at_down = pl.ds(pl.multiple_of(16 * ((z + step) % 8), 16), 16)
        out = [remote(b_main.at[8, core, at_up], b_main.at[8, core, at_up], s_rs.at[0, step], s_rr.at[0, step], up)]
        if step < 3:
            out.append(remote(b_main.at[8, core, at_down], b_main.at[8, core, at_down],
                              s_rs.at[1, step], s_rr.at[1, step], down))
        return out

    main, rest = {}, []

    def share(r, chunk):
        at = chunks[chunk]
        return remote(b_main.at[r, core, :, at], b_main.at[r, core, :, at], s_ks.at[r, chunk], s_kr.at[r, chunk], sibling)

    def next_rest(step):
        if step:
            got(rest[step - 1])
        rest.append(start(rest_copies(step)))

    def next_main(step, chunk):
        if step:
            got(main[step - 1, chunk])
        main[step, chunk] = start(main_copies(step, chunk))
        for r in sorted({step, (8 - step) % 8}):
            share(r, chunk).start()

    def repack(half):
        own_a(half).wait()
        pl.loop(1, 16)(lambda i: a_copy(half, i).wait_recv())

        @pl.loop(0, 8)
        def _(s):
            v = a_recv[half, pl.ds(2 * s, 2)].astype(jnp.float32)
            a_mat[half, pl.ds(pl.multiple_of(48 * s, 48), 48), :] = v.reshape(48, kt * LANES).astype(jnp.bfloat16)

    def arrived(r):
        for chunk in range(2):
            share(r, chunk).wait_recv()

    def product(v, halves):
        total = None
        for half in halves:
            both = jnp.concatenate([b_main[v, half], b_main[8 - v, half]], axis=0)
            part = lax.dot_general(a_mat[half], both, (((1,), (1,)), ((), ())), preferred_element_type=jnp.float32)
            total = part if total is None else total + part
        for n, r in enumerate((v, 8 - v)):
            tile = total[:, n * LANES:(n + 1) * LANES].reshape(4, 4, 24, LANES)
            odd = r % 2
            for i in range(4):
                for j in range(4):
                    a, b = i + odd * (j - i), j + odd * (i - j)
                    c_part[r, a, b] = c_part[r, a, b] + tile[i, j] if halves == (1,) else tile[i, j]

    def for_pair(v, act):
        act(v)

        @pl.when(v < 4)
        def _():
            act(8 - v)

    def line_peer(r, k, odd):
        return (((x + k * (1 - odd)) % 4) * 2 + core, z * 4 + (y + k * odd) % 4)

    def first_copies(r):
        odd = r % 2
        mine = x + odd * (y - x)
        return [remote(c_part.at[r, (mine + k) % 4], c_in1.at[r, k - 1], s_c1s.at[r, k - 1], s_c1r.at[r, k - 1],
                       line_peer(r, k, odd)) for k in (1, 3, 2)]

    def second_copies(r):
        odd = r % 2
        mine = y + odd * (x - y)
        return [remote(c_sum.at[r, (mine + k) % 4], c_in2.at[r, k - 1], s_c2s.at[r, k - 1], s_c2r.at[r, k - 1],
                       line_peer(r, k, 1 - odd)) for k in (1, 3, 2)]

    def send_second(r):
        got(first_copies(r))
        c_sum[r] = c_part[r, x + r % 2 * (y - x)] + c_in1[r, 0] + c_in1[r, 1] + c_in1[r, 2]
        start(second_copies(r))

    def finish(r):
        got(second_copies(r))
        total = c_sum[r, y + r % 2 * (x - y)] + c_in2[r, 0] + c_in2[r, 1] + c_in2[r, 2]
        c_out[r // 8 * 8 + (1 - r // 8) * ((z + r) % 8)] = total

    pack_quads(0)
    send_a(0)
    lay_out_first()
    next_main(0, 0)
    pack_quads(1)
    send_a(1)
    lay_out_second()
    next_main(0, 1)
    next_rest(0)
    next_main(1, 0)
    next_rest(1)
    next_main(1, 1)
    next_rest(2)
    next_main(2, 0)
    next_rest(3)
    next_main(2, 1)
    got(rest[3])
    for chunk in range(2):
        share(8, chunk).start()
    repack(0)

    @pl.loop(0, 3)
    def _(v):
        for_pair(v, arrived)
        product(v, (0,))

    next_main(3, 0)
    next_main(3, 1)
    repack(1)

    @pl.loop(0, 7)
    def _(v):
        @pl.when(v == 4)
        def _():
            for chunk in range(2):
                got(main[3, chunk])
                share(4, chunk).start()

        @pl.when(v < 3)
        def _():
            product(v, (1,))

        @pl.when((v >= 3) & (v < 5))
        def _():
            for_pair(v, arrived)
            product(v, (0, 1))

        @pl.when(v < 5)
        def _():
            for_pair(v, lambda r: start(first_copies(r)))

        @pl.when((v >= 1) & (v < 6))
        def _():
            for_pair(v - 1, send_second)

        @pl.when(v >= 2)
        def _():
            for_pair(v - 2, finish)

    size_b = jnp.int32(0)
    for h in range(NIRR):
        size_b = jnp.where(window[1] == h, sizes[h], size_b)
    for t in range(8):
        o_ref[:, 144 * t:144 * t + 128] = c_out[t]
        o_ref[:, 144 * t + 128:144 * t + 144] = c_out[8, :, 16 * t:16 * t + 16]
    slot = lax.broadcasted_iota(jnp.int32, (24, 8 * 144), 1)
    o_ref[...] = jnp.where(slot % NB < size_b, o_ref[...], 0.0)

    @pl.loop(1, 16)
    def _(i):
        for half in range(2):
            a_copy(half, i).wait_send()
            b_copy(half, i).wait_send()

    @pl.loop(0, 9)
    def _(r):
        for c in first_copies(r) + second_copies(r) + [share(r, 0), share(r, 1)]:
            c.wait_send()

    for copies in rest + list(main.values()):
        for c in copies:
            c.wait_send()


def ladder_call(kt, collective_id, table, window, sizes, amplitudes, b_packed):
    kh = kt * LANES
    bf, f32 = jnp.bfloat16, jnp.float32
    dma = pltpu.SemaphoreType.DMA
    smem = pl.BlockSpec(memory_space=pltpu.SMEM)
    hbm = pl.BlockSpec(memory_space=pl.ANY)
    return pl.pallas_call(
        functools.partial(kernel, kt),
        out_shape=jax.ShapeDtypeStruct((24, 8 * 144), f32),
        in_specs=[smem] * 3 + [hbm] * 2,
        out_specs=pl.BlockSpec(memory_space=pltpu.VMEM),
        scratch_shapes=[
            pltpu.VMEM((24, NIRR * NB * NB), bf),
            pltpu.VMEM((NIRR * NQ * 3 + 1, 24, LANES), f32),
            pltpu.VMEM((QUAD, QUAD), bf),
            pltpu.VMEM((2, 16, 24, kh), bf),
            pltpu.VMEM((16, EARLY, 40, LANES), bf),
            pltpu.VMEM((16, WT - EARLY, 40, LANES), bf),
            pltpu.VMEM((144, LANES), f32),
            pltpu.VMEM((2, 16, 24, kh), bf),
            pltpu.VMEM((2, 384, kh), bf),
            pltpu.VMEM((9, 2, 128, kh), bf),
            pltpu.VMEM((9, 4, 4, 24, LANES), f32),
            pltpu.VMEM((9, 3, 4, 24, LANES), f32),
            pltpu.VMEM((9, 4, 24, LANES), f32),
            pltpu.VMEM((9, 3, 24, LANES), f32),
            pltpu.VMEM((9, 24, LANES), f32),
            dma((10,)), dma((2, 16)), dma((2, 16)), dma((2, 16)), dma((2, 16)),
            dma((2, 4, 2)), dma((2, 4, 2)), dma((2, 4)), dma((2, 4)), dma((9, 2)), dma((9, 2)),
            dma((9, 3)), dma((9, 3)), dma((9, 3)), dma((9, 3)),
        ],
        compiler_params=pltpu.CompilerParams(
            collective_id=collective_id, has_side_effects=True, vmem_limit_bytes=60 * 2**20),
    )(table, window, sizes, amplitudes, b_packed)


def shards(amplitudes, integrals, block_sizes, window_irreps):
    b_packed, table, width = deal_call(block_sizes, window_irreps, integrals)
    which = sum((width[0] > w).astype(jnp.int32) for w in WIDTHS[:-1])
    calls = [functools.partial(ladder_call, w, i) for i, w in enumerate(WIDTHS)]
    return lax.switch(which, calls, table, window_irreps, block_sizes, amplitudes, b_packed)


def solution(mesh):
    placed = (P(("row", "col"), None), P("col", "row"), P(), P())
    return jax.shard_map(
        shards, mesh=mesh, in_specs=placed, out_specs=P(("row", "col"), None), check_vma=False
    )
```
